128 devices in a mesh: ctx: 8 (over z, x_hi), head: 8 (over x_lo, y), grp: 2 (over core).
Axes of the slice: x: 4 (x_hi: 2, x_lo: 2; x = x_hi * 2 + x_lo), y: 4, z: 4, core: 2. Of those that a mesh axis runs over, the one named last changes fastest.
Arguments:
- prompt_queries: bfloat16 [8192, 8192], P(('ctx', 'grp'), 'head'), may hold values from -16 to 16
- rotated_prompt_keys: bfloat16 [8192, 1024], P(('ctx', 'grp'), 'head'), may hold values from -12 to 12
- prompt_value_rows: bfloat16 [8192, 1024], P(('ctx', 'grp'), 'head'), may hold values from -12 to 12
- continuation_queries: bfloat16 [768, 8192], P(('ctx', 'grp'), 'head'), may hold values from -16 to 16
- prefix_len: int32 [768], replicated, may hold values from 2 to 8192
- out_weight: bfloat16 [8192, 8192], P('head', ('ctx', 'grp')), may hold values from -0.0625 to 0.0625
Outputs:
- prompt_context: bfloat16 [8192, 8192], P(('ctx', 'grp'), 'head')
- mixed: bfloat16 [768, 8192], P('head', ('ctx', 'grp'))
The draws below stay inside these ranges and needn't reach their ends.
Inputs may be any that keep to these rules, and one draw needn't show every extreme that they name: Continuation b reads prompt positions 0 to prefix_len[b] - 1.
All inputs are finite; a program needn't handle non-finite values.
Results may differ from the reference program's by a relative error of at most 0.018.
Values may be sent and summed in bfloat16 or wider, within the bound.
A program may use at most 64 MiB of HBM per device.

```python
import jax
import jax.numpy as jnp
from jax import lax

D = 8192
QUERY_HEADS = 64
KEY_VALUE_HEADS = 8
HEAD_WIDTH = 128
PROMPT_LENGTH = 8192
CONTINUATION_NUM = 768


def drawn_queries(key, salt, total_rows, heads):
    random_jitter = jnp.clip(1.6 * jax.random.normal(jax.random.fold_in(key, salt), (total_rows, heads, HEAD_WIDTH), jnp.float32), -8.0, 8.0)
    return random_jitter.reshape(total_rows, heads * HEAD_WIDTH).astype(jnp.bfloat16)


def draw_prompt_queries(key, part):
    return drawn_queries(key, 11, PROMPT_LENGTH, QUERY_HEADS)


def draw_continuation_queries(key, part):
    return drawn_queries(key, 13, CONTINUATION_NUM, QUERY_HEADS)


def draw_rotated_prompt_keys(key, part):
    random_jitter = jnp.clip(1.6 * jax.random.normal(jax.random.fold_in(key, 12), (PROMPT_LENGTH, KEY_VALUE_HEADS, HEAD_WIDTH), jnp.float32), -8.0, 8.0)
    return random_jitter.reshape(PROMPT_LENGTH, KEY_VALUE_HEADS * HEAD_WIDTH).astype(jnp.bfloat16)


def plant(entries, rng, least, high):
    index_at = [jax.random.randint(jax.random.fold_in(rng, axis), (), 0, length) for axis, length in enumerate(entries.shape)]
    longest = entries.shape.index(max(entries.shape))
    beside = index_at[:longest] + [(index_at[longest] + 1) % entries.shape[longest]] + index_at[longest + 1:]
    return entries.at[tuple(index_at)].set(least).at[tuple(beside)].set(high)


def block_scale(key, extent, shards, low, high):
    def one(axis_at, parts):
        heights = jax.random.uniform(jax.random.fold_in(jax.random.fold_in(key, 6), axis_at), (parts,), jnp.float32, low / len(shards), high / len(shards))
        return jnp.repeat(jnp.exp(heights), extent[axis_at] // parts).reshape((-1,) + (1,) * (len(extent) - axis_at - 1))

    loudness = one(*shards[0])
    for cut in shards[1:]:
        loudness = loudness * one(*cut)
    return loudness


def bell_draw(rng, extent, deviation, limit, pieces=(), kind=jnp.bfloat16):
    entries = deviation * jax.random.normal(rng, extent, jnp.float32)
    if pieces:
        entries = entries * block_scale(rng, extent, pieces, -0.22, 0.18)
    return jnp.clip(entries, -limit, limit).astype(kind)


def setup_inputs(seed: int = 0) -> dict:
    seeds = jax.random.split(jax.random.key(seed), 7)
    prompt_queries = draw_prompt_queries(jax.random.fold_in(seeds[6], 71), 0)
    rotated_prompt_keys = draw_rotated_prompt_keys(jax.random.fold_in(seeds[6], 71), 0)
    prompt_value_rows = bell_draw(seeds[2], (PROMPT_LENGTH, KEY_VALUE_HEADS * HEAD_WIDTH), 2.0, 12.0, ((0, 16), (1, 8)))
    continuation_queries = draw_continuation_queries(jax.random.fold_in(seeds[6], 71), 0)
    prefix_len = plant(jax.random.randint(seeds[4], (CONTINUATION_NUM,), 2, PROMPT_LENGTH + 1), jax.random.fold_in(seeds[4], 1), 2, PROMPT_LENGTH).astype(jnp.int32)
    out_weight = bell_draw(seeds[5], (QUERY_HEADS * HEAD_WIDTH, D), (QUERY_HEADS * HEAD_WIDTH) ** -0.5, 0.0625, ((0, 8), (1, 16)))
    return dict(prompt_queries=prompt_queries, rotated_prompt_keys=rotated_prompt_keys, prompt_value_rows=prompt_value_rows, continuation_queries=continuation_queries, prefix_len=prefix_len, out_weight=out_weight)


NEG = -1e30


def softmax_rows(queries, key_rows, value_rows, allowed):
    scores = jnp.dot(queries.astype(jnp.float32), key_rows.astype(jnp.float32).T) * (HEAD_WIDTH ** -0.5)
    scores = jnp.where(allowed, scores, NEG)
    highest = jnp.max(scores, axis=1, keepdims=True)
    powers = jnp.exp(scores - highest)
    totals = jnp.sum(powers, axis=1, keepdims=True)
    rounded = lax.optimization_barrier(powers.astype(jnp.bfloat16))
    weighted = jnp.dot(rounded.astype(jnp.float32), value_rows.astype(jnp.float32))
    return (weighted / totals).astype(jnp.bfloat16)


def reference(prompt_queries, rotated_prompt_keys, prompt_value_rows, continuation_queries, prefix_len, out_weight):
    query_group_count = QUERY_HEADS // KEY_VALUE_HEADS
    places = jnp.arange(PROMPT_LENGTH, dtype=jnp.int32)
    expanded_key_heads = rotated_prompt_keys.reshape(PROMPT_LENGTH, KEY_VALUE_HEADS, HEAD_WIDTH).transpose(1, 0, 2)
    expanded_value_heads = prompt_value_rows.reshape(PROMPT_LENGTH, KEY_VALUE_HEADS, HEAD_WIDTH).transpose(1, 0, 2)

    def prompt_head(triple):
        queries, key_rows, value_rows = triple
        allowed = places[None, :] <= places[:, None]
        return softmax_rows(queries, key_rows, value_rows, allowed)

    query_heads = prompt_queries.reshape(PROMPT_LENGTH, QUERY_HEADS, HEAD_WIDTH).transpose(1, 0, 2)
    prompt_out = lax.map(prompt_head, (query_heads, jnp.repeat(expanded_key_heads, query_group_count, axis=0), jnp.repeat(expanded_value_heads, query_group_count, axis=0)))
    prompt_context = prompt_out.transpose(1, 0, 2).reshape(PROMPT_LENGTH, QUERY_HEADS * HEAD_WIDTH)

    lengths_rows = jnp.repeat(prefix_len, query_group_count)

    def decode_head(triple):
        queries, key_rows, value_rows = triple
        allowed = places[None, :] < lengths_rows[:, None]
        return softmax_rows(queries, key_rows, value_rows, allowed)

    continuation_rows = continuation_queries.reshape(CONTINUATION_NUM, KEY_VALUE_HEADS, query_group_count, HEAD_WIDTH).transpose(1, 0, 2, 3).reshape(KEY_VALUE_HEADS, CONTINUATION_NUM * query_group_count, HEAD_WIDTH)
    continuation_output = lax.map(decode_head, (continuation_rows, expanded_key_heads, expanded_value_heads))
    continuation_context = continuation_output.reshape(KEY_VALUE_HEADS, CONTINUATION_NUM, query_group_count, HEAD_WIDTH).transpose(1, 0, 2, 3).reshape(CONTINUATION_NUM, QUERY_HEADS * HEAD_WIDTH)
    mixed = jnp.dot(continuation_context.astype(jnp.float32), out_weight.astype(jnp.float32)).astype(jnp.bfloat16)
    return (prompt_context, mixed)
```

```python
import math

import jax
import jax.numpy as jnp
from jax import lax
from jax.experimental import pallas as pl
from jax.experimental.pallas import tpu as pltpu
from jax.sharding import PartitionSpec as P

MESH = pl.DeviceIdType.MESH
HEAD_WIDTH = 128
HEADS = 8
BLOCK = 512
PAIR = 2 * BLOCK
CHUNK = 128
PROMPT = 8192
CONT = 768
OWN = 48
NEG = -1e30
FACTOR = HEAD_WIDTH**-0.5 * math.log2(math.e)


def lanes(h):
    return pl.ds(h * HEAD_WIDTH, HEAD_WIDTH)


def fold(queries, keys, values, limits, base, states):
    width = keys.shape[0]
    scores = [
        lax.dot_general(q, keys, (((1,), (1,)), ((), ())), preferred_element_type=jnp.float32)
        for q in queries
    ]
    results = []
    for s, limit, (m_old, acc_old) in zip(scores, limits, states):
        if limit is not None:
            place = lax.broadcasted_iota(jnp.int32, s.shape, 1)
            if limit.shape[1] != width:
                limit = jnp.concatenate([limit] * (width // limit.shape[1]), axis=1)
            s = jnp.where(place < limit - base, s, NEG)
        m_new = jnp.maximum(m_old, jnp.max(s, axis=1, keepdims=True))
        wide = jnp.concatenate([m_new] * (width // HEAD_WIDTH), axis=1)
        p = jnp.exp2((s - wide) * FACTOR).astype(jnp.bfloat16)
        shrink = jnp.exp2((m_old - m_new) * FACTOR)
        o = jnp.dot(p, values, preferred_element_type=jnp.float32)
        results.append((m_new, acc_old * jnp.concatenate([shrink, shrink], axis=1) + o))
    return results


def kernel(
    q_ref, k_ref, v_ref, dq_ref, len_ref, w_ref,
    ctx_ref, mix_ref,
    qall, kall, vall, acc, mx, dacc, dmx, done, dctx, dall, part, parts,
    direct_send, direct_recv, forward_send, forward_recv,
    q_send, q_recv, back_send, back_recv, front_sem,
    d_send, d_recv, part_send, part_recv,
):
    c, h, g = lax.axis_index("ctx"), lax.axis_index("head"), lax.axis_index("grp")
    z, xh = c // 2, c % 2
    other = 1 - g
    mirror = 2 * (3 - z) + xh

    def step_ctx(s):
        flip, turn = s % 2, s // 2
        z_met = jnp.where(
            turn == 0, z, jnp.where(turn == 1, z + 1 - 2 * (z % 2), jnp.where(turn == 2, 3 - z, (z + 2) % 4))
        )
        x_met = jnp.where(flip == 0, xh, 1 - xh)
        return 2 * z_met + x_met

    barrier = pltpu.get_barrier_semaphore()

    def greet(s, carry):
        met = step_ctx(s)
        pl.semaphore_signal(barrier, inc=1, device_id=(met, h, other), device_id_type=MESH)

        @pl.when(s > 0)
        def _():
            pl.semaphore_signal(barrier, inc=1, device_id=(met, h, g), device_id_type=MESH)
            pl.semaphore_signal(barrier, inc=1, device_id=(c, (h + s) % 8, g), device_id_type=MESH)

        return carry

    lax.fori_loop(0, 8, greet, 0)

    mine = pl.ds(pl.multiple_of(c * PAIR + g * BLOCK, BLOCK), BLOCK)
    vall[:, HEAD_WIDTH:] = jnp.ones((PROMPT, HEAD_WIDTH), jnp.bfloat16)
    kall[mine, :] = k_ref[...]
    vall[mine, :HEAD_WIDTH] = v_ref[...]
    qall[: BLOCK // 2, :] = q_ref[: BLOCK // 2, :]
    acc[...] = jnp.zeros_like(acc)
    mx[...] = jnp.full_like(mx, NEG)
    dacc[...] = jnp.zeros_like(dacc)
    dmx[...] = jnp.full_like(dmx, NEG)
    pl.semaphore_wait(barrier, 22)

    def rows_of(met, core):
        return pl.ds(pl.multiple_of(met * PAIR + core * BLOCK, BLOCK), BLOCK)

    def direct(s):
        met = step_ctx(s)
        return [
            pltpu.make_async_remote_copy(
                src_ref=src, dst_ref=dst, send_sem=direct_send.at[i, s], recv_sem=direct_recv.at[i, s],
                device_id=(met, h, g), device_id_type=MESH,
            )
            for i, src, dst in ((0, k_ref, kall.at[mine]), (1, v_ref, vall.at[mine, pl.ds(0, HEAD_WIDTH)]))
        ]

    def forward(s):
        rows = rows_of(step_ctx(s), g)
        return [
            pltpu.make_async_remote_copy(
                src_ref=ref, dst_ref=ref, send_sem=forward_send.at[i, s], recv_sem=forward_recv.at[i, s],
                device_id=(c, h, other), device_id_type=MESH,
            )
            for i, ref in ((0, kall.at[rows]), (1, vall.at[rows, pl.ds(0, HEAD_WIDTH)]))
        ]

    def query_copy(n):
        rows = pl.ds(BLOCK // 2 + n * CHUNK, CHUNK)
        return pltpu.make_async_remote_copy(
            src_ref=q_ref.at[rows], dst_ref=qall.at[rows], send_sem=q_send.at[n], recv_sem=q_recv.at[n],
            device_id=(mirror, h, other), device_id_type=MESH,
        )

    for copy in forward(0):
        copy.start()
    query_copy(0).start()

    def send_block(s, carry):
        for copy in direct(s):
            copy.start()
        return carry

    lax.fori_loop(1, 8, send_block, 0)
    query_copy(1).start()

    def owner(n):
        front = n < 2
        return jnp.where(front, c, mirror), jnp.where(front, g, other)

    def chunk_state(n, t):
        return pl.ds(pl.multiple_of(n * (HEADS * CHUNK) + t * (HEADS * CHUNK // 2), 512), HEADS * CHUNK // 2)

    def fold_chunk(n, pair, width, diagonal):
        rows = pl.ds(pl.multiple_of(n * CHUNK, CHUNK), CHUNK)
        span = pl.ds(pl.multiple_of(pair * PAIR, PAIR), width)
        queries = [
            jnp.concatenate([qall[rows, lanes(4 * t + k)] for k in range(4)], axis=0) for t in range(2)
        ]
        if diagonal:
            start = owner(n)[1] * BLOCK + n * CHUNK + 1
            limit = start + lax.broadcasted_iota(jnp.int32, (512, width), 0) % CHUNK
            limits = [limit, limit]
        else:
            limits = [None, None]
        places = [chunk_state(n, t) for t in range(2)]
        states = [(mx[at, :], acc[at, :]) for at in places]
        results = fold(queries, kall[span, :], vall[span, :], limits, 0, states)
        for at, (m_new, acc_new) in zip(places, results):
            mx[at, :] = m_new
            acc[at, :] = acc_new

    def fold_diagonal(n):
        pair, core = owner(n)

        @pl.when(core == 0)
        def _():
            fold_chunk(n, pair, BLOCK, True)

        @pl.when(core == 1)
        def _():
            fold_chunk(n, pair, PAIR, True)

    def fold_decode(pair):
        span = pl.ds(pl.multiple_of(pair * PAIR, PAIR), PAIR)
        queries = [
            jnp.concatenate([dq_ref[:, lanes(4 * t + k)] for k in range(4)], axis=0) for t in range(2)
        ]
        limit = jnp.concatenate([len_ref[...]] * 4, axis=0)
        places = [pl.ds(t * 4 * OWN, 4 * OWN) for t in range(2)]
        states = [(dmx[at, :], dacc[at, :]) for at in places]
        results = fold(queries, kall[span, :], vall[span, :], [limit, limit], pair * PAIR, states)
        for at, (m_new, acc_new) in zip(places, results):
            dmx[at, :] = m_new
            dacc[at, :] = acc_new

    def back_copy(n):
        rows = pl.ds(pl.multiple_of(n * CHUNK, CHUNK), CHUNK)
        return pltpu.make_async_remote_copy(
            src_ref=done.at[rows], dst_ref=ctx_ref.at[rows], send_sem=back_send.at[n - 2],
            recv_sem=back_recv.at[n - 2], device_id=(mirror, h, other), device_id_type=MESH,
        )

    def front_copy(n):
        rows = pl.ds(pl.multiple_of(n * CHUNK, CHUNK), CHUNK)
        return pltpu.make_async_copy(done.at[rows], ctx_ref.at[rows], front_sem.at[n])

    def finish_chunk(n):
        rows = pl.ds(pl.multiple_of(n * CHUNK, CHUNK), CHUNK)
        for k in range(HEADS):
            at = pl.ds(pl.multiple_of(n * (HEADS * CHUNK) + k * CHUNK, CHUNK), CHUNK)
            done[rows, lanes(k)] = (acc[at, :HEAD_WIDTH] / acc[at, HEAD_WIDTH:]).astype(jnp.bfloat16)

        @pl.when(n < 2)
        def _():
            front_copy(n).start()

        @pl.when(n >= 2)
        def _():
            back_copy(n).start()

    early = jnp.where(z >= 2, 0, 2)
    early_pair = owner(early)[0]

    def arrive(s, carry):
        @pl.when((s > 0) & (s < 8))
        def _():
            for copy in direct(s):
                copy.wait_recv()
            for copy in forward(s):
                copy.start()

        @pl.when(s > 0)
        def _():
            now = s - 1
            pair = step_ctx(now)
            for copy in forward(now):
                copy.wait_recv()
            fold_decode(pair)

            @pl.when((now == 0) & (z < 2))
            def _():
                query_copy(0).wait_recv()

            @pl.when(pair < early_pair)
            def _():
                fold_chunk(early, pair, PAIR, False)

            @pl.when(pair == early_pair)
            def _():
                fold_diagonal(early)

        return carry

    lax.fori_loop(1, 9, arrive, 0)

    def own_rows(met, core):
        return pl.ds(pl.multiple_of((2 * met + core) * OWN, 16), OWN)

    for k in range(HEADS):
        at = pl.ds(k * OWN, OWN)
        dctx[:, lanes(k)] = (dacc[at, :HEAD_WIDTH] / dacc[at, HEAD_WIDTH:]).astype(jnp.bfloat16)
    dall[own_rows(c, g), :] = dctx[...]

    def decode_copy(s, flip):
        return pltpu.make_async_remote_copy(
            src_ref=dctx, dst_ref=dall.at[own_rows(c, g)], send_sem=d_send.at[flip, s], recv_sem=d_recv.at[flip, s],
            device_id=(step_ctx(s), h, other if flip else g), device_id_type=MESH,
        )

    def send_decode(s, carry):
        @pl.when(s > 0)
        def _():
            decode_copy(s, 0).start()

        decode_copy(s, 1).start()
        return carry

    lax.fori_loop(0, 8, send_decode, 0)
    finish_chunk(early)

    @pl.when(z >= 2)
    def _():
        query_copy(0).wait_recv()

    query_copy(1).wait_recv()

    def part_copy(s):
        to = (h + s) % 8
        return pltpu.make_async_remote_copy(
            src_ref=part.at[pl.ds(pl.multiple_of(to * 96, 32), 96)], dst_ref=parts.at[s],
            send_sem=part_send.at[s], recv_sem=part_recv.at[s],
            device_id=(c, to, g), device_id_type=MESH,
        )

    def project():
        def arrived(s, carry):
            @pl.when(s > 0)
            def _():
                decode_copy(s, 0).wait_recv()

            decode_copy(s, 1).wait_recv()
            return carry

        lax.fori_loop(0, 8, arrived, 0)
        for n in range(2):
            part[:, n * 256 : (n + 1) * 256] = jnp.dot(
                dall[...], w_ref[:, n * 256 : (n + 1) * 256], preferred_element_type=jnp.float32
            ).astype(jnp.bfloat16)

        def send(s, carry):
            part_copy(s).start()
            return carry

        lax.fori_loop(1, 8, send, 0)

    def late(n, carry):
        chunk = jnp.where(z >= 2, jnp.where(n == 2, 1, n + 2), (n + 3) % 4)
        pair_end = owner(chunk)[0]

        def one(pair, inner):
            fold_chunk(chunk, pair, PAIR, False)
            return inner

        lax.fori_loop(0, pair_end, one, 0)
        fold_diagonal(chunk)
        finish_chunk(chunk)

        @pl.when(n == 2)
        def _():
            project()

        return carry

    lax.fori_loop(0, 3, late, 0)

    def add(s, carry):
        part_copy(s).wait_recv()
        return carry

    lax.fori_loop(1, 8, add, 0)
    total = part[pl.ds(pl.multiple_of(h * 96, 32), 96), :].astype(jnp.float32)
    for s in range(1, 8):
        total = total + parts[s].astype(jnp.float32)
    mix_ref[...] = total.astype(jnp.bfloat16)

    for n in range(2):
        front_copy(n).wait()
        back_copy(n + 2).wait_recv()
        back_copy(n + 2).wait_send()
        query_copy(n).wait_send()

    def drain(s, carry):
        for copy in forward(s):
            copy.wait_send()
        decode_copy(s, 1).wait_send()

        @pl.when(s > 0)
        def _():
            for copy in direct(s):
                copy.wait_send()
            decode_copy(s, 0).wait_send()
            part_copy(s).wait_send()

        return carry

    lax.fori_loop(0, 8, drain, 0)


def local(q, k, v, dq, prefix_len, w):
    index = 2 * lax.axis_index("ctx") + lax.axis_index("grp")
    own = lax.dynamic_slice_in_dim(prefix_len, index * OWN, OWN, 0)
    own = jnp.broadcast_to(own[:, None], (OWN, HEAD_WIDTH))
    vmem = pl.BlockSpec(memory_space=pltpu.VMEM)
    dma = pltpu.SemaphoreType.DMA
    bf16, f32 = jnp.bfloat16, jnp.float32
    return pl.pallas_call(
        kernel,
        out_shape=(
            jax.ShapeDtypeStruct((BLOCK, HEADS * HEAD_WIDTH), bf16),
            jax.ShapeDtypeStruct((96, 512), bf16),
        ),
        in_specs=[vmem] * 6,
        out_specs=(pl.BlockSpec(memory_space=pl.ANY), vmem),
        scratch_shapes=[
            pltpu.VMEM((BLOCK, HEADS * HEAD_WIDTH), bf16),
            pltpu.VMEM((PROMPT, HEAD_WIDTH), bf16),
            pltpu.VMEM((PROMPT, 2 * HEAD_WIDTH), bf16),
            pltpu.VMEM((BLOCK * HEADS, 2 * HEAD_WIDTH), f32),
            pltpu.VMEM((BLOCK * HEADS, HEAD_WIDTH), f32),
            pltpu.VMEM((OWN * HEADS, 2 * HEAD_WIDTH), f32),
            pltpu.VMEM((OWN * HEADS, HEAD_WIDTH), f32),
            pltpu.VMEM((BLOCK, HEADS * HEAD_WIDTH), bf16),
            pltpu.VMEM((OWN, HEADS * HEAD_WIDTH), bf16),
            pltpu.VMEM((CONT, HEADS * HEAD_WIDTH), bf16),
            pltpu.VMEM((CONT, 512), bf16),
            pltpu.VMEM((8, 96, 512), bf16),
            dma((2, 8)), dma((2, 8)), dma((2, 8)), dma((2, 8)),
            dma((2,)), dma((2,)), dma((2,)), dma((2,)), dma((2,)),
            dma((2, 8)), dma((2, 8)), dma((8,)), dma((8,)),
        ],
        compiler_params=pltpu.CompilerParams(
            collective_id=0, has_side_effects=True, vmem_limit_bytes=56 << 20
        ),
    )(q, k, v, dq, own, w)


def solution(mesh):
    in_specs = (
        P(("ctx", "grp"), "head"),
        P(("ctx", "grp"), "head"),
        P(("ctx", "grp"), "head"),
        P(("ctx", "grp"), "head"),
        P(),
        P("head", ("ctx", "grp")),
    )
    out_specs = (P(("ctx", "grp"), "head"), P("head", ("ctx", "grp")))
    return jax.shard_map(local, mesh=mesh, in_specs=in_specs, out_specs=out_specs, check_vma=False)
```

```python
import math

import jax
import jax.numpy as jnp
from jax import lax
from jax.experimental import pallas as pl
from jax.experimental.pallas import tpu as pltpu
from jax.sharding import PartitionSpec as P

MESH = pl.DeviceIdType.MESH
HEAD_WIDTH = 128
HEADS = 8
BLOCK = 512
PAIR = 2 * BLOCK
CHUNK = 128
PROMPT = 8192
CONT = 768
OWN = 48
NEG = -1e30
FACTOR = HEAD_WIDTH**-0.5 * math.log2(math.e)


def lanes(h):
    return pl.ds(h * HEAD_WIDTH, HEAD_WIDTH)


def fold(queries, keys, values, limits, base, states):
    width = keys.shape[0]
    scores = [
        lax.dot_general(q, keys, (((1,), (1,)), ((), ())), preferred_element_type=jnp.float32)
        for q in queries
    ]
    results = []
    for s, limit, (m_old, acc_old) in zip(scores, limits, states):
        if limit is not None:
            place = lax.broadcasted_iota(jnp.int32, s.shape, 1)
            if limit.shape[1] != width:
                limit = jnp.concatenate([limit] * (width // limit.shape[1]), axis=1)
            s = jnp.where(place < limit - base, s, NEG)
        m_new = jnp.maximum(m_old, jnp.max(s, axis=1, keepdims=True))
        wide = jnp.concatenate([m_new] * (width // HEAD_WIDTH), axis=1)
        p = jnp.exp2((s - wide) * FACTOR).astype(jnp.bfloat16)
        shrink = jnp.exp2((m_old - m_new) * FACTOR)
        o = jnp.dot(p, values, preferred_element_type=jnp.float32)
        results.append((m_new, acc_old * jnp.concatenate([shrink, shrink], axis=1) + o))
    return results


def kernel(
    q_ref, k_ref, v_ref, dq_hbm, len_ref, w_hbm,
    ctx_ref, mix_ref,
    qall, kall, vall, acc, mx, dacc, dmx, done, dall, part, parts, dq_ref, lens, w_ref,
    load_sem, direct_send, direct_recv, forward_send, forward_recv,
    q_send, q_recv, back_send, back_recv, front_sem,
    d_send, d_recv, part_send, part_recv,
):
    c, h, g = lax.axis_index("ctx"), lax.axis_index("head"), lax.axis_index("grp")
    z, xh = c // 2, c % 2
    other = 1 - g
    mirror = 2 * (3 - z) + xh

    def met_at(s):
        flip, turn = s % 2, s // 2
        z_met = jnp.where(
            turn == 0, z, jnp.where(turn == 1, z + 1 - 2 * (z % 2), jnp.where(turn == 2, 3 - z, (z + 2) % 4))
        )
        x_met = jnp.where(flip == 0, xh, 1 - xh)
        return 2 * z_met + x_met

    barrier = pltpu.get_barrier_semaphore()

    def greet(s, carry):
        pl.semaphore_signal(barrier, inc=1, device_id=(met_at(s), h, g), device_id_type=MESH)
        pl.semaphore_signal(barrier, inc=1, device_id=(c, (h + s) % 8, g), device_id_type=MESH)
        return carry

    pl.semaphore_signal(barrier, inc=1, device_id=(c, h, other), device_id_type=MESH)
    pl.semaphore_signal(barrier, inc=1, device_id=(mirror, h, other), device_id_type=MESH)
    lax.fori_loop(1, 8, greet, 0)

    mine = pl.ds(pl.multiple_of(c * PAIR + g * BLOCK, BLOCK), BLOCK)
    front = pl.ds(0, BLOCK // 2)
    loads = [
        pltpu.make_async_copy(src, dst, load_sem.at[i])
        for i, (src, dst) in enumerate(
            (
                (k_ref, kall.at[mine]),
                (v_ref, vall.at[mine, pl.ds(0, HEAD_WIDTH)]),
                (dq_hbm, dq_ref),
                (q_ref.at[front], qall.at[front]),
                (w_hbm, w_ref),
            )
        )
    ]
    for copy in loads:
        copy.start()
    vall[:, HEAD_WIDTH:] = jnp.ones((PROMPT, HEAD_WIDTH), jnp.bfloat16)
    acc[...] = jnp.zeros_like(acc)
    mx[...] = jnp.full_like(mx, NEG)
    dacc[...] = jnp.zeros_like(dacc)
    dmx[...] = jnp.full_like(dmx, NEG)
    for copy in loads[:2]:
        copy.wait()
    pl.semaphore_wait(barrier, 16)

    def rows_of(met):
        return pl.ds(pl.multiple_of(met * PAIR + g * BLOCK, BLOCK), BLOCK)

    def copies(rows, to, core, send, recv, s):
        return [
            pltpu.make_async_remote_copy(
                src_ref=ref, dst_ref=ref, send_sem=send.at[i, s], recv_sem=recv.at[i, s],
                device_id=(to, h, core), device_id_type=MESH,
            )
            for i, ref in ((0, kall.at[rows]), (1, vall.at[rows, pl.ds(0, HEAD_WIDTH)]))
        ]

    def sent(s, origin, to):
        return copies(rows_of(origin), to, g, direct_send, direct_recv, s)

    def came(s):
        return copies(rows_of(met_at(s)), c, other, direct_send, direct_recv, s)

    def forward(s):
        return copies(rows_of(met_at(s)), c, other, forward_send, forward_recv, s)

    def query_copy(n):
        rows = pl.ds(BLOCK // 2 + n * CHUNK, CHUNK)
        return pltpu.make_async_remote_copy(
            src_ref=q_ref.at[rows], dst_ref=qall.at[rows], send_sem=q_send.at[n], recv_sem=q_recv.at[n],
            device_id=(mirror, h, other), device_id_type=MESH,
        )

    for s in (2, 1, 4):
        for copy in sent(s, c, met_at(s)):
            copy.start()
    for copy in forward(0):
        copy.start()
    query_copy(0).start()
    for copy in sent(6, c, met_at(6)):
        copy.start()

    base = (2 * c + g) * OWN
    for n in range(OWN // 8):
        row = lax.broadcasted_iota(jnp.int32, (8, HEAD_WIDTH), 0)
        value = jnp.zeros((8, HEAD_WIDTH), jnp.int32)
        for r in range(8):
            value = jnp.where(row == r, len_ref[base + n * 8 + r], value)
        lens[n * 8 : n * 8 + 8, :] = value
    for copy in loads[2:]:
        copy.wait()

    def owner(n):
        front = n < 2
        return jnp.where(front, c, mirror), jnp.where(front, g, other)

    def chunk_state(n, t):
        return pl.ds(pl.multiple_of(n * (HEADS * CHUNK) + t * (HEADS * CHUNK // 2), 512), HEADS * CHUNK // 2)

    def fold_chunk(n, pair, width, diagonal):
        rows = pl.ds(pl.multiple_of(n * CHUNK, CHUNK), CHUNK)
        span = pl.ds(pl.multiple_of(pair * PAIR, PAIR), width)
        queries = [
            jnp.concatenate([qall[rows, lanes(4 * t + k)] for k in range(4)], axis=0) for t in range(2)
        ]
        if diagonal:
            start = owner(n)[1] * BLOCK + n * CHUNK + 1
            limit = start + lax.broadcasted_iota(jnp.int32, (512, width), 0) % CHUNK
            limits = [limit, limit]
        else:
            limits = [None, None]
        places = [chunk_state(n, t) for t in range(2)]
        states = [(mx[at, :], acc[at, :]) for at in places]
        results = fold(queries, kall[span, :], vall[span, :], limits, 0, states)
        for at, (m_new, acc_new) in zip(places, results):
            mx[at, :] = m_new
            acc[at, :] = acc_new

    def fold_diagonal(n):
        pair, core = owner(n)

        @pl.when(core == 0)
        def _():
            fold_chunk(n, pair, BLOCK, True)

        @pl.when(core == 1)
        def _():
            fold_chunk(n, pair, PAIR, True)

    def fold_decode(pair):
        span = pl.ds(pl.multiple_of(pair * PAIR, PAIR), PAIR)
        queries = [
            jnp.concatenate([dq_ref[:, lanes(4 * t + k)] for k in range(4)], axis=0) for t in range(2)
        ]
        limit = jnp.concatenate([lens[...]] * 4, axis=0)
        places = [pl.ds(t * 4 * OWN, 4 * OWN) for t in range(2)]
        states = [(dmx[at, :], dacc[at, :]) for at in places]
        results = fold(queries, kall[span, :], vall[span, :], [limit, limit], pair * PAIR, states)
        for at, (m_new, acc_new) in zip(places, results):
            dmx[at, :] = m_new
            dacc[at, :] = acc_new

    def back_copy(n):
        rows = pl.ds(pl.multiple_of(n * CHUNK, CHUNK), CHUNK)
        return pltpu.make_async_remote_copy(
            src_ref=done.at[rows], dst_ref=ctx_ref.at[rows], send_sem=back_send.at[n - 2],
            recv_sem=back_recv.at[n - 2], device_id=(mirror, h, other), device_id_type=MESH,
        )

    def front_copy(n):
        rows = pl.ds(pl.multiple_of(n * CHUNK, CHUNK), CHUNK)
        return pltpu.make_async_copy(done.at[rows], ctx_ref.at[rows], front_sem.at[n])

    def finish_chunk(n):
        rows = pl.ds(pl.multiple_of(n * CHUNK, CHUNK), CHUNK)
        for k in range(HEADS):
            at = pl.ds(pl.multiple_of(n * (HEADS * CHUNK) + k * CHUNK, CHUNK), CHUNK)
            done[rows, lanes(k)] = (acc[at, :HEAD_WIDTH] / acc[at, HEAD_WIDTH:]).astype(jnp.bfloat16)

        @pl.when(n < 2)
        def _():
            front_copy(n).start()

        @pl.when(n >= 2)
        def _():
            back_copy(n).start()

    early = jnp.where(z >= 2, 0, 2)
    early_pair = owner(early)[0]

    def own_rows(met):
        return pl.ds(pl.multiple_of((2 * met + g) * OWN, 16), OWN)

    def decode_copy(s, met, to, core, i):
        rows = own_rows(met)
        return pltpu.make_async_remote_copy(
            src_ref=dall.at[rows], dst_ref=dall.at[rows], send_sem=d_send.at[i, s], recv_sem=d_recv.at[i, s],
            device_id=(to, h, core), device_id_type=MESH,
        )

    def decode_direct(s):
        return decode_copy(s, c, met_at(s), g, 0)

    def decode_came(s):
        return decode_copy(s, met_at(s), c, other, 0)

    def decode_forward(s):
        return decode_copy(s, met_at(s), c, other, 1)

    def finish_decode():
        for k in range(HEADS):
            at = pl.ds(k * OWN, OWN)
            dall[own_rows(c), lanes(k)] = (dacc[at, :HEAD_WIDTH] / dacc[at, HEAD_WIDTH:]).astype(jnp.bfloat16)

        def send(s, carry):
            decode_direct(s).start()
            return carry

        lax.fori_loop(1, 8, send, 0)
        decode_forward(0).start()

    def in_turn(k):
        return jnp.where(k == 1, 2, jnp.where(k == 2, 1, jnp.where(k == 3, 4, jnp.where(k == 4, 6, jnp.where(k == 5, 3, jnp.where(k == 6, 5, k))))))

    def arrive(k, carry):
        s = in_turn(k)

        @pl.when(k < 8)
        def _():
            for copy in came(s):
                copy.wait_recv()
            for relayed, via, to in ((3, 1, 2), (5, 4, 1), (7, 6, 1)):

                @pl.when(s == via)
                def _():
                    for copy in sent(relayed, met_at(via), met_at(to)):
                        copy.start()

            for copy in forward(s):
                copy.start()

        @pl.when(k == 4)
        def _():
            query_copy(1).start()

        now = in_turn(k - 1)
        pair = met_at(now)
        for copy in forward(now):
            copy.wait_recv()
        fold_decode(pair)

        @pl.when((k == 1) & (z < 2))
        def _():
            query_copy(0).wait_recv()

        @pl.when(k == 8)
        def _():
            finish_decode()

        @pl.when(pair < early_pair)
        def _():
            fold_chunk(early, pair, PAIR, False)

        @pl.when(pair == early_pair)
        def _():
            fold_diagonal(early)

        return carry

    lax.fori_loop(1, 9, arrive, 0)
    finish_chunk(early)

    @pl.when(z >= 2)
    def _():
        query_copy(0).wait_recv()

    query_copy(1).wait_recv()

    def part_copy(s):
        to = (h + s) % 8
        return pltpu.make_async_remote_copy(
            src_ref=part.at[pl.ds(pl.multiple_of(to * 96, 32), 96)], dst_ref=parts.at[s],
            send_sem=part_send.at[s], recv_sem=part_recv.at[s],
            device_id=(c, to, g), device_id_type=MESH,
        )

    def hand_on():
        def one(s, carry):
            decode_came(s).wait_recv()
            decode_forward(s).start()
            return carry

        lax.fori_loop(1, 8, one, 0)

    def project():
        def arrived(s, carry):
            decode_forward(s).wait_recv()
            return carry

        lax.fori_loop(0, 8, arrived, 0)
        for n in range(2):
            part[:, n * 256 : (n + 1) * 256] = jnp.dot(
                dall[...], w_ref[:, n * 256 : (n + 1) * 256], preferred_element_type=jnp.float32
            ).astype(jnp.bfloat16)

        def send(s, carry):
            part_copy(s).start()
            return carry

        lax.fori_loop(1, 8, send, 0)

    def late(n, count):
        chunk = jnp.where(z >= 2, jnp.where(n == 2, 1, n + 2), (n + 3) % 4)
        pair_end = owner(chunk)[0]

        def one(pair, inner):
            @pl.when(count + pair == 5)
            def _():
                hand_on()

            @pl.when(count + pair == 7)
            def _():
                project()

            @pl.when(pair < pair_end)
            def _():
                fold_chunk(chunk, pair, PAIR, False)

            @pl.when(pair == pair_end)
            def _():
                fold_diagonal(chunk)

            return inner

        lax.fori_loop(0, pair_end + 1, one, 0)
        finish_chunk(chunk)
        return count + pair_end + 1

    lax.fori_loop(0, 3, late, 0)

    def add(s, carry):
        part_copy(s).wait_recv()
        return carry

    lax.fori_loop(1, 8, add, 0)
    total = part[pl.ds(pl.multiple_of(h * 96, 32), 96), :].astype(jnp.float32)
    for s in range(1, 8):
        total = total + parts[s].astype(jnp.float32)
    mix_ref[...] = total.astype(jnp.bfloat16)

    for n in range(2):
        front_copy(n).wait()
        back_copy(n + 2).wait_recv()
        back_copy(n + 2).wait_send()
        query_copy(n).wait_send()

    def drain(s, carry):
        for copy in forward(s):
            copy.wait_send()
        decode_forward(s).wait_send()

        @pl.when(s > 0)
        def _():
            for copy in came(s):
                copy.wait_send()
            decode_came(s).wait_send()
            part_copy(s).wait_send()

        return carry

    lax.fori_loop(0, 8, drain, 0)


def local(q, k, v, dq, prefix_len, w):
    anywhere = pl.BlockSpec(memory_space=pl.ANY)
    dma = pltpu.SemaphoreType.DMA
    bf16, f32 = jnp.bfloat16, jnp.float32
    return pl.pallas_call(
        kernel,
        out_shape=(
            jax.ShapeDtypeStruct((BLOCK, HEADS * HEAD_WIDTH), bf16),
            jax.ShapeDtypeStruct((96, 512), bf16),
        ),
        in_specs=[anywhere] * 4 + [pl.BlockSpec(memory_space=pltpu.SMEM), anywhere],
        out_specs=(anywhere, pl.BlockSpec(memory_space=pltpu.VMEM)),
        scratch_shapes=[
            pltpu.VMEM((BLOCK, HEADS * HEAD_WIDTH), bf16),
            pltpu.VMEM((PROMPT, HEAD_WIDTH), bf16),
            pltpu.VMEM((PROMPT, 2 * HEAD_WIDTH), bf16),
            pltpu.VMEM((BLOCK * HEADS, 2 * HEAD_WIDTH), f32),
            pltpu.VMEM((BLOCK * HEADS, HEAD_WIDTH), f32),
            pltpu.VMEM((OWN * HEADS, 2 * HEAD_WIDTH), f32),
            pltpu.VMEM((OWN * HEADS, HEAD_WIDTH), f32),
            pltpu.VMEM((BLOCK, HEADS * HEAD_WIDTH), bf16),
            pltpu.VMEM((CONT, HEADS * HEAD_WIDTH), bf16),
            pltpu.VMEM((CONT, 512), bf16),
            pltpu.VMEM((8, 96, 512), bf16),
            pltpu.VMEM((OWN, HEADS * HEAD_WIDTH), bf16),
            pltpu.VMEM((OWN, HEAD_WIDTH), jnp.int32),
            pltpu.VMEM((HEADS * HEAD_WIDTH, 512), bf16),
            dma((5,)),
            dma((2, 8)), dma((2, 8)), dma((2, 8)), dma((2, 8)),
            dma((2,)), dma((2,)), dma((2,)), dma((2,)), dma((2,)),
            dma((2, 8)), dma((2, 8)), dma((8,)), dma((8,)),
        ],
        compiler_params=pltpu.CompilerParams(
            collective_id=0, has_side_effects=True, vmem_limit_bytes=56 << 20
        ),
    )(q, k, v, dq, prefix_len, w)


def solution(mesh):
    in_specs = (
        P(("ctx", "grp"), "head"),
        P(("ctx", "grp"), "head"),
        P(("ctx", "grp"), "head"),
        P(("ctx", "grp"), "head"),
        P(),
        P("head", ("ctx", "grp")),
    )
    out_specs = (P(("ctx", "grp"), "head"), P("head", ("ctx", "grp")))
    return jax.shard_map(local, mesh=mesh, in_specs=in_specs, out_specs=out_specs, check_vma=False)
```

```python
import math

import jax
import jax.numpy as jnp
from jax import lax
from jax.experimental import pallas as pl
from jax.experimental.pallas import tpu as pltpu
from jax.sharding import PartitionSpec as P

MESH = pl.DeviceIdType.MESH
HEAD_WIDTH = 128
HEADS = 8
BLOCK = 512
PAIR = 2 * BLOCK
CHUNK = 128
PROMPT = 8192
CONT = 768
OWN = 48
NEG = -1e30
FACTOR = HEAD_WIDTH**-0.5 * math.log2(math.e)


def lanes(h):
    return pl.ds(h * HEAD_WIDTH, HEAD_WIDTH)


def fold(queries, keys, values, limits, base, states):
    width = keys.shape[0]
    scores = [
        lax.dot_general(q, keys, (((1,), (1,)), ((), ())), preferred_element_type=jnp.float32)
        for q in queries
    ]
    results = []
    for s, limit, (m_old, acc_old) in zip(scores, limits, states):
        if limit is not None:
            place = lax.broadcasted_iota(jnp.int32, s.shape, 1)
            if limit.shape[1] != width:
                limit = jnp.concatenate([limit] * (width // limit.shape[1]), axis=1)
            s = jnp.where(place < limit - base, s, NEG)
        m_new = jnp.maximum(m_old, jnp.max(s, axis=1, keepdims=True))
        wide = jnp.concatenate([m_new] * (width // HEAD_WIDTH), axis=1)
        p = jnp.exp2((s - wide) * FACTOR).astype(jnp.bfloat16)
        shrink = jnp.exp2((m_old - m_new) * FACTOR)
        o = jnp.dot(p, values, preferred_element_type=jnp.float32)
        results.append((m_new, acc_old * jnp.concatenate([shrink, shrink], axis=1) + o))
    return results


def kernel(
    q_ref, k_ref, v_ref, dq_hbm, len_ref, w_hbm,
    ctx_ref, mix_ref,
    qall, kall, vall, acc, mx, dacc, dmx, done, dall, part, parts, dq_ref, lens, w_ref,
    load_sem, direct_send, direct_recv, forward_send, forward_recv,
    q_send, q_recv, back_send, back_recv, front_sem,
    d_send, d_recv, part_send, part_recv,
):
    c, h, g = lax.axis_index("ctx"), lax.axis_index("head"), lax.axis_index("grp")
    z, xh = c // 2, c % 2
    other = 1 - g
    mirror = 2 * (3 - z) + xh

    def met_at(s):
        flip, turn = s % 2, s // 2
        z_met = jnp.where(
            turn == 0, z, jnp.where(turn == 1, z + 1 - 2 * (z % 2), jnp.where(turn == 2, 3 - z, (z + 2) % 4))
        )
        x_met = jnp.where(flip == 0, xh, 1 - xh)
        return 2 * z_met + x_met

    barrier = pltpu.get_barrier_semaphore()

    def greet(s, carry):
        pl.semaphore_signal(barrier, inc=1, device_id=(met_at(s), h, g), device_id_type=MESH)
        pl.semaphore_signal(barrier, inc=1, device_id=(c, (h + s) % 8, g), device_id_type=MESH)
        return carry

    pl.semaphore_signal(barrier, inc=1, device_id=(c, h, other), device_id_type=MESH)
    pl.semaphore_signal(barrier, inc=1, device_id=(mirror, h, other), device_id_type=MESH)
    lax.fori_loop(1, 8, greet, 0)

    mine = pl.ds(pl.multiple_of(c * PAIR + g * BLOCK, BLOCK), BLOCK)
    front = pl.ds(0, BLOCK // 2)
    loads = [
        pltpu.make_async_copy(src, dst, load_sem.at[i])
        for i, (src, dst) in enumerate(
            (
                (k_ref, kall.at[mine]),
                (v_ref, vall.at[mine, pl.ds(0, HEAD_WIDTH)]),
                (dq_hbm, dq_ref),
                (q_ref.at[front], qall.at[front]),
                (w_hbm, w_ref),
            )
        )
    ]
    for copy in loads:
        copy.start()
    vall[:, HEAD_WIDTH:] = jnp.ones((PROMPT, HEAD_WIDTH), jnp.bfloat16)
    acc[...] = jnp.zeros_like(acc)
    mx[...] = jnp.full_like(mx, NEG)
    dacc[...] = jnp.zeros_like(dacc)
    dmx[...] = jnp.full_like(dmx, NEG)
    for copy in loads[:2]:
        copy.wait()
    pl.semaphore_wait(barrier, 16)

    def rows_of(met):
        return pl.ds(pl.multiple_of(met * PAIR + g * BLOCK, BLOCK), BLOCK)

    def copies(rows, to, core, send, recv, s):
        return [
            pltpu.make_async_remote_copy(
                src_ref=ref, dst_ref=ref, send_sem=send.at[i, s], recv_sem=recv.at[i, s],
                device_id=(to, h, core), device_id_type=MESH,
            )
            for i, ref in ((0, kall.at[rows]), (1, vall.at[rows, pl.ds(0, HEAD_WIDTH)]))
        ]

    def sent(s, origin, to):
        return copies(rows_of(origin), to, g, direct_send, direct_recv, s)

    def came(s):
        return copies(rows_of(met_at(s)), c, other, direct_send, direct_recv, s)

    def forward(s):
        return copies(rows_of(met_at(s)), c, other, forward_send, forward_recv, s)

    def query_copy(n):
        rows = pl.ds(BLOCK // 2 + n * CHUNK, CHUNK)
        return pltpu.make_async_remote_copy(
            src_ref=q_ref.at[rows], dst_ref=qall.at[rows], send_sem=q_send.at[n], recv_sem=q_recv.at[n],
            device_id=(mirror, h, other), device_id_type=MESH,
        )

    for s in (4, 1, 2):
        for copy in sent(s, c, met_at(s)):
            copy.start()
    for copy in forward(0):
        copy.start()

    base = (2 * c + g) * OWN
    for n in range(OWN // 8):
        row = lax.broadcasted_iota(jnp.int32, (8, HEAD_WIDTH), 0)
        value = jnp.zeros((8, HEAD_WIDTH), jnp.int32)
        for r in range(8):
            value = jnp.where(row == r, len_ref[base + n * 8 + r], value)
        lens[n * 8 : n * 8 + 8, :] = value
    for copy in loads[2:]:
        copy.wait()

    def owner(n):
        front = n < 2
        return jnp.where(front, c, mirror), jnp.where(front, g, other)

    def chunk_state(n, t):
        return pl.ds(pl.multiple_of(n * (HEADS * CHUNK) + t * (HEADS * CHUNK // 2), 512), HEADS * CHUNK // 2)

    def fold_chunk(n, pair, width, diagonal):
        rows = pl.ds(pl.multiple_of(n * CHUNK, CHUNK), CHUNK)
        span = pl.ds(pl.multiple_of(pair * PAIR, PAIR), width)
        queries = [
            jnp.concatenate([qall[rows, lanes(4 * t + k)] for k in range(4)], axis=0) for t in range(2)
        ]
        if diagonal:
            start = owner(n)[1] * BLOCK + n * CHUNK + 1
            limit = start + lax.broadcasted_iota(jnp.int32, (512, width), 0) % CHUNK
            limits = [limit, limit]
        else:
            limits = [None, None]
        places = [chunk_state(n, t) for t in range(2)]
        states = [(mx[at, :], acc[at, :]) for at in places]
        results = fold(queries, kall[span, :], vall[span, :], limits, 0, states)
        for at, (m_new, acc_new) in zip(places, results):
            mx[at, :] = m_new
            acc[at, :] = acc_new

    def fold_diagonal(n):
        pair, core = owner(n)

        @pl.when(core == 0)
        def _():
            fold_chunk(n, pair, BLOCK, True)

        @pl.when(core == 1)
        def _():
            fold_chunk(n, pair, PAIR, True)

    def fold_decode(pair):
        span = pl.ds(pl.multiple_of(pair * PAIR, PAIR), PAIR)
        queries = [
            jnp.concatenate([dq_ref[:, lanes(4 * t + k)] for k in range(4)], axis=0) for t in range(2)
        ]
        limit = jnp.concatenate([lens[...]] * 4, axis=0)
        places = [pl.ds(t * 4 * OWN, 4 * OWN) for t in range(2)]
        states = [(dmx[at, :], dacc[at, :]) for at in places]
        results = fold(queries, kall[span, :], vall[span, :], [limit, limit], pair * PAIR, states)
        for at, (m_new, acc_new) in zip(places, results):
            dmx[at, :] = m_new
            dacc[at, :] = acc_new

    def back_copy(n):
        rows = pl.ds(pl.multiple_of(n * CHUNK, CHUNK), CHUNK)
        return pltpu.make_async_remote_copy(
            src_ref=done.at[rows], dst_ref=ctx_ref.at[rows], send_sem=back_send.at[n - 2],
            recv_sem=back_recv.at[n - 2], device_id=(mirror, h, other), device_id_type=MESH,
        )

    def front_copy(n):
        rows = pl.ds(pl.multiple_of(n * CHUNK, CHUNK), CHUNK)
        return pltpu.make_async_copy(done.at[rows], ctx_ref.at[rows], front_sem.at[n])

    def finish_chunk(n):
        rows = pl.ds(pl.multiple_of(n * CHUNK, CHUNK), CHUNK)
        for k in range(HEADS):
            at = pl.ds(pl.multiple_of(n * (HEADS * CHUNK) + k * CHUNK, CHUNK), CHUNK)
            done[rows, lanes(k)] = (acc[at, :HEAD_WIDTH] / acc[at, HEAD_WIDTH:]).astype(jnp.bfloat16)

        @pl.when(n < 2)
        def _():
            front_copy(n).start()

        @pl.when(n >= 2)
        def _():
            back_copy(n).start()

    early = jnp.where(z >= 2, 0, 2)
    early_pair = owner(early)[0]

    def own_rows(met):
        return pl.ds(pl.multiple_of((2 * met + g) * OWN, 16), OWN)

    def decode_copy(s, met, to, core, i):
        rows = own_rows(met)
        return pltpu.make_async_remote_copy(
            src_ref=dall.at[rows], dst_ref=dall.at[rows], send_sem=d_send.at[i, s], recv_sem=d_recv.at[i, s],
            device_id=(to, h, core), device_id_type=MESH,
        )

    def decode_direct(s):
        return decode_copy(s, c, met_at(s), g, 0)

    def decode_came(s):
        return decode_copy(s, met_at(s), c, other, 0)

    def decode_forward(s):
        return decode_copy(s, met_at(s), c, other, 1)

    def finish_decode():
        for k in range(HEADS):
            at = pl.ds(k * OWN, OWN)
            dall[own_rows(c), lanes(k)] = (dacc[at, :HEAD_WIDTH] / dacc[at, HEAD_WIDTH:]).astype(jnp.bfloat16)

        def send(s, carry):
            decode_direct(s).start()
            return carry

        lax.fori_loop(1, 8, send, 0)
        decode_forward(0).start()

    def in_turn(k):
        return jnp.where(k == 1, 4, jnp.where(k == 2, 1, jnp.where(k == 3, 2, jnp.where(k == 4, 6, jnp.where(k == 6, 3, k)))))

    def relay(s, origin, to):
        for copy in sent(s, met_at(origin), met_at(to)):
            copy.start()

    def take(k):
        s = in_turn(k)
        for copy in came(s):
            copy.wait_recv()

        @pl.when(s == 4)
        def _():
            relay(6, 4, 2)
            relay(5, 4, 1)
            query_copy(0).start()

        @pl.when(s == 6)
        def _():
            relay(7, 6, 1)
            relay(3, 1, 2)
            query_copy(1).start()

        for copy in forward(s):
            copy.start()

    def early_tile(e, carry):
        pair = met_at(in_turn(e))

        @pl.when(pair < early_pair)
        def _():
            fold_chunk(early, pair, PAIR, False)

        @pl.when(pair == early_pair)
        def _():
            fold_diagonal(early)

        return carry

    def early_until(k):
        return jnp.where(z >= 2, jnp.minimum(k + 1, 5), jnp.where(k < 3, 0, jnp.where(k == 3, 2, 4)))

    def step(k, carry):
        first = jnp.where(k == 0, 1, jnp.where(k == 1, 1, k + 2))
        last = jnp.where(k == 0, 1, jnp.minimum(k + 3, 8))

        def ahead(n, inner):
            take(n)
            return inner

        lax.fori_loop(first, last, ahead, 0)
        s = in_turn(k)
        for copy in forward(s):
            copy.wait_recv()
        fold_decode(met_at(s))

        @pl.when(k == 7)
        def _():
            finish_decode()

        @pl.when((k == 3) & (z < 2))
        def _():
            query_copy(0).wait_recv()

        lax.fori_loop(jnp.where(k == 0, 0, early_until(k - 1)), early_until(k), early_tile, 0)
        return carry

    lax.fori_loop(0, 8, step, 0)
    lax.fori_loop(early_until(7), 8, early_tile, 0)
    finish_chunk(early)

    @pl.when(z >= 2)
    def _():
        query_copy(0).wait_recv()

    query_copy(1).wait_recv()

    def part_copy(s):
        to = (h + s) % 8
        return pltpu.make_async_remote_copy(
            src_ref=part.at[pl.ds(pl.multiple_of(to * 96, 32), 96)], dst_ref=parts.at[s],
            send_sem=part_send.at[s], recv_sem=part_recv.at[s],
            device_id=(c, to, g), device_id_type=MESH,
        )

    def hand_on():
        def one(s, carry):
            decode_came(s).wait_recv()
            decode_forward(s).start()
            return carry

        lax.fori_loop(1, 8, one, 0)

    def project():
        def arrived(s, carry):
            decode_forward(s).wait_recv()
            return carry

        lax.fori_loop(0, 8, arrived, 0)
        for n in range(2):
            part[:, n * 256 : (n + 1) * 256] = jnp.dot(
                dall[...], w_ref[:, n * 256 : (n + 1) * 256], preferred_element_type=jnp.float32
            ).astype(jnp.bfloat16)

        def send(s, carry):
            part_copy(s).start()
            return carry

        lax.fori_loop(1, 8, send, 0)

    def late(n, count):
        chunk = jnp.where(z >= 2, jnp.where(n == 2, 1, n + 2), (n + 3) % 4)
        pair_end = owner(chunk)[0]

        def one(pair, inner):
            @pl.when(count + pair == 3)
            def _():
                hand_on()

            @pl.when(count + pair == 5)
            def _():
                project()

            @pl.when(pair < pair_end)
            def _():
                fold_chunk(chunk, pair, PAIR, False)

            @pl.when(pair == pair_end)
            def _():
                fold_diagonal(chunk)

            return inner

        lax.fori_loop(0, pair_end + 1, one, 0)
        finish_chunk(chunk)
        return count + pair_end + 1

    lax.fori_loop(0, 3, late, 0)

    def add(s, carry):
        part_copy(s).wait_recv()
        return carry

    lax.fori_loop(1, 8, add, 0)
    total = part[pl.ds(pl.multiple_of(h * 96, 32), 96), :].astype(jnp.float32)
    for s in range(1, 8):
        total = total + parts[s].astype(jnp.float32)
    mix_ref[...] = total.astype(jnp.bfloat16)

    for n in range(2):
        front_copy(n).wait()
        back_copy(n + 2).wait_recv()
        back_copy(n + 2).wait_send()
        query_copy(n).wait_send()

    def drain(s, carry):
        for copy in forward(s):
            copy.wait_send()
        decode_forward(s).wait_send()

        @pl.when(s > 0)
        def _():
            for copy in came(s):
                copy.wait_send()
            decode_came(s).wait_send()
            part_copy(s).wait_send()

        return carry

    lax.fori_loop(0, 8, drain, 0)


def local(q, k, v, dq, prefix_len, w):
    anywhere = pl.BlockSpec(memory_space=pl.ANY)
    dma = pltpu.SemaphoreType.DMA
    bf16, f32 = jnp.bfloat16, jnp.float32
    return pl.pallas_call(
        kernel,
        out_shape=(
            jax.ShapeDtypeStruct((BLOCK, HEADS * HEAD_WIDTH), bf16),
            jax.ShapeDtypeStruct((96, 512), bf16),
        ),
        in_specs=[anywhere] * 4 + [pl.BlockSpec(memory_space=pltpu.SMEM), anywhere],
        out_specs=(anywhere, pl.BlockSpec(memory_space=pltpu.VMEM)),
        scratch_shapes=[
            pltpu.VMEM((BLOCK, HEADS * HEAD_WIDTH), bf16),
            pltpu.VMEM((PROMPT, HEAD_WIDTH), bf16),
            pltpu.VMEM((PROMPT, 2 * HEAD_WIDTH), bf16),
            pltpu.VMEM((BLOCK * HEADS, 2 * HEAD_WIDTH), f32),
            pltpu.VMEM((BLOCK * HEADS, HEAD_WIDTH), f32),
            pltpu.VMEM((OWN * HEADS, 2 * HEAD_WIDTH), f32),
            pltpu.VMEM((OWN * HEADS, HEAD_WIDTH), f32),
            pltpu.VMEM((BLOCK, HEADS * HEAD_WIDTH), bf16),
            pltpu.VMEM((CONT, HEADS * HEAD_WIDTH), bf16),
            pltpu.VMEM((CONT, 512), bf16),
            pltpu.VMEM((8, 96, 512), bf16),
            pltpu.VMEM((OWN, HEADS * HEAD_WIDTH), bf16),
            pltpu.VMEM((OWN, HEAD_WIDTH), jnp.int32),
            pltpu.VMEM((HEADS * HEAD_WIDTH, 512), bf16),
            dma((5,)),
            dma((2, 8)), dma((2, 8)), dma((2, 8)), dma((2, 8)),
            dma((2,)), dma((2,)), dma((2,)), dma((2,)), dma((2,)),
            dma((2, 8)), dma((2, 8)), dma((8,)), dma((8,)),
        ],
        compiler_params=pltpu.CompilerParams(
            collective_id=0, has_side_effects=True, vmem_limit_bytes=56 << 20
        ),
    )(q, k, v, dq, prefix_len, w)


def solution(mesh):
    in_specs = (
        P(("ctx", "grp"), "head"),
        P(("ctx", "grp"), "head"),
        P(("ctx", "grp"), "head"),
        P(("ctx", "grp"), "head"),
        P(),
        P("head", ("ctx", "grp")),
    )
    out_specs = (P(("ctx", "grp"), "head"), P("head", ("ctx", "grp")))
    return jax.shard_map(local, mesh=mesh, in_specs=in_specs, out_specs=out_specs, check_vma=False)
```

```python
import math

import jax
import jax.numpy as jnp
from jax import lax
from jax.experimental import pallas as pl
from jax.experimental.pallas import tpu as pltpu
from jax.sharding import PartitionSpec as P

MESH = pl.DeviceIdType.MESH
HEAD_WIDTH = 128
HEADS = 8
BLOCK = 512
PAIR = 2 * BLOCK
CHUNK = 128
CHUNKS = BLOCK // CHUNK
MOVED = CHUNKS - 1
PROMPT = 8192
CONT = 768
OWN = 48
NEG = -1e30
FACTOR = HEAD_WIDTH**-0.5 * math.log2(math.e)


def lanes(h):
    return pl.ds(h * HEAD_WIDTH, HEAD_WIDTH)


def fold(queries, keys, values, limits, base, states):
    width = keys.shape[0]
    scores = [
        lax.dot_general(q, keys, (((1,), (1,)), ((), ())), preferred_element_type=jnp.float32)
        for q in queries
    ]
    results = []
    for s, limit, (m_old, acc_old) in zip(scores, limits, states):
        if limit is not None:
            place = lax.broadcasted_iota(jnp.int32, s.shape, 1)
            if limit.shape[1] != width:
                limit = jnp.concatenate([limit] * (width // limit.shape[1]), axis=1)
            s = jnp.where(place < limit - base, s, NEG)
        m_new = jnp.maximum(m_old, jnp.max(s, axis=1, keepdims=True))
        wide = jnp.concatenate([m_new] * (width // HEAD_WIDTH), axis=1)
        p = jnp.exp2((s - wide) * FACTOR).astype(jnp.bfloat16)
        shrink = jnp.exp2((m_old - m_new) * FACTOR)
        o = jnp.dot(p, values, preferred_element_type=jnp.float32)
        results.append((m_new, acc_old * jnp.concatenate([shrink, shrink], axis=1) + o))
    return results


def kernel(
    q_ref, k_ref, v_ref, dq_hbm, len_ref, w_hbm,
    ctx_ref, mix_ref,
    qall, kall, vall, acc, mx, dacc, dmx, done, dall, part, parts, dq_ref, lens, w_ref,
    load_sem, direct_send, direct_recv, forward_send, forward_recv,
    q_send, q_recv, back_send, back_recv, front_sem,
    d_send, d_recv, part_send, part_recv,
):
    c, h, g = lax.axis_index("ctx"), lax.axis_index("head"), lax.axis_index("grp")
    z, xh = c // 2, c % 2
    other = 1 - g
    mirror = 2 * (3 - z) + xh

    def met_at(s):
        flip, turn = s % 2, s // 2
        z_met = jnp.where(
            turn == 0, z, jnp.where(turn == 1, z + 1 - 2 * (z % 2), jnp.where(turn == 2, 3 - z, (z + 2) % 4))
        )
        x_met = jnp.where(flip == 0, xh, 1 - xh)
        return 2 * z_met + x_met

    barrier = pltpu.get_barrier_semaphore()

    def greet(s, carry):
        pl.semaphore_signal(barrier, inc=1, device_id=(met_at(s), h, g), device_id_type=MESH)
        pl.semaphore_signal(barrier, inc=1, device_id=(c, (h + s) % 8, g), device_id_type=MESH)
        return carry

    pl.semaphore_signal(barrier, inc=1, device_id=(c, h, other), device_id_type=MESH)
    pl.semaphore_signal(barrier, inc=1, device_id=(mirror, h, other), device_id_type=MESH)
    lax.fori_loop(1, 8, greet, 0)

    mine = pl.ds(pl.multiple_of(c * PAIR + g * BLOCK, BLOCK), BLOCK)
    front = pl.ds(0, BLOCK)
    loads = [
        pltpu.make_async_copy(src, dst, load_sem.at[i])
        for i, (src, dst) in enumerate(
            (
                (k_ref, kall.at[mine]),
                (v_ref, vall.at[mine, pl.ds(0, HEAD_WIDTH)]),
                (dq_hbm, dq_ref),
                (q_ref, qall.at[front]),
                (w_hbm, w_ref),
            )
        )
    ]
    for copy in loads:
        copy.start()
    vall[:, HEAD_WIDTH:] = jnp.ones((PROMPT, HEAD_WIDTH), jnp.bfloat16)
    acc[...] = jnp.zeros_like(acc)
    mx[...] = jnp.full_like(mx, NEG)
    dacc[...] = jnp.zeros_like(dacc)
    dmx[...] = jnp.full_like(dmx, NEG)
    for copy in loads[:2]:
        copy.wait()
    pl.semaphore_wait(barrier, 16)

    def rows_of(met):
        return pl.ds(pl.multiple_of(met * PAIR + g * BLOCK, BLOCK), BLOCK)

    def copy_of(i, rows, to, core, send, recv, s):
        ref = kall.at[rows] if i == 0 else vall.at[rows, pl.ds(0, HEAD_WIDTH)]
        return pltpu.make_async_remote_copy(
            src_ref=ref, dst_ref=ref, send_sem=send.at[i, s], recv_sem=recv.at[i, s],
            device_id=(to, h, core), device_id_type=MESH,
        )

    def sent(s, origin, to, i):
        return copy_of(i, rows_of(origin), to, g, direct_send, direct_recv, s)

    def came(s, i):
        return copy_of(i, rows_of(met_at(s)), c, other, direct_send, direct_recv, s)

    def forward(s, i):
        return copy_of(i, rows_of(met_at(s)), c, other, forward_send, forward_recv, s)

    def query_copy():
        return pltpu.make_async_remote_copy(
            src_ref=q_ref.at[pl.ds(MOVED * CHUNK, CHUNK)], dst_ref=qall.at[pl.ds(BLOCK, CHUNK)], send_sem=q_send, recv_sem=q_recv,
            device_id=(mirror, h, other), device_id_type=MESH,
        )

    for i in range(2):
        for s in (4, 1, 2):
            sent(s, c, met_at(s), i).start()
    for i in range(2):
        forward(0, i).start()

    base = (2 * c + g) * OWN
    for n in range(OWN // 8):
        row = lax.broadcasted_iota(jnp.int32, (8, HEAD_WIDTH), 0)
        value = jnp.zeros((8, HEAD_WIDTH), jnp.int32)
        for r in range(8):
            value = jnp.where(row == r, len_ref[base + n * 8 + r], value)
        lens[n * 8 : n * 8 + 8, :] = value
    for copy in loads[2:]:
        copy.wait()

    def owner(n):
        front = n < CHUNKS
        return jnp.where(front, c, mirror), jnp.where(front, g, other)

    def chunk_state(n, t):
        return pl.ds(pl.multiple_of(n * (HEADS * CHUNK) + t * (HEADS * CHUNK // 2), 512), HEADS * CHUNK // 2)

    def fold_chunk(n, pair, width, diagonal):
        rows = pl.ds(pl.multiple_of(n * CHUNK, CHUNK), CHUNK)
        span = pl.ds(pl.multiple_of(pair * PAIR, PAIR), width)
        queries = [
            jnp.concatenate([qall[rows, lanes(4 * t + k)] for k in range(4)], axis=0) for t in range(2)
        ]
        if diagonal:
            start = owner(n)[1] * BLOCK + jnp.where(n == CHUNKS, MOVED, n) * CHUNK + 1
            limit = start + lax.broadcasted_iota(jnp.int32, (512, width), 0) % CHUNK
            limits = [limit, limit]
        else:
            limits = [None, None]
        places = [chunk_state(n, t) for t in range(2)]
        states = [(mx[at, :], acc[at, :]) for at in places]
        results = fold(queries, kall[span, :], vall[span, :], limits, 0, states)
        for at, (m_new, acc_new) in zip(places, results):
            mx[at, :] = m_new
            acc[at, :] = acc_new

    def fold_diagonal(n):
        pair, core = owner(n)

        @pl.when(core == 0)
        def _():
            fold_chunk(n, pair, BLOCK, True)

        @pl.when(core == 1)
        def _():
            fold_chunk(n, pair, PAIR, True)

    def fold_decode(pair):
        span = pl.ds(pl.multiple_of(pair * PAIR, PAIR), PAIR)
        queries = [
            jnp.concatenate([dq_ref[:, lanes(4 * t + k)] for k in range(4)], axis=0) for t in range(2)
        ]
        limit = jnp.concatenate([lens[...]] * 4, axis=0)
        places = [pl.ds(t * 4 * OWN, 4 * OWN) for t in range(2)]
        states = [(dmx[at, :], dacc[at, :]) for at in places]
        results = fold(queries, kall[span, :], vall[span, :], [limit, limit], pair * PAIR, states)
        for at, (m_new, acc_new) in zip(places, results):
            dmx[at, :] = m_new
            dacc[at, :] = acc_new

    def back_copy():
        return pltpu.make_async_remote_copy(
            src_ref=done.at[pl.ds(BLOCK, CHUNK)], dst_ref=ctx_ref.at[pl.ds(MOVED * CHUNK, CHUNK)], send_sem=back_send, recv_sem=back_recv,
            device_id=(mirror, h, other), device_id_type=MESH,
        )

    def front_copy(n):
        rows = pl.ds(pl.multiple_of(n * CHUNK, CHUNK), CHUNK)
        return pltpu.make_async_copy(done.at[rows], ctx_ref.at[rows], front_sem.at[n])

    def finish_chunk(n):
        rows = pl.ds(pl.multiple_of(n * CHUNK, CHUNK), CHUNK)
        for k in range(HEADS):
            at = pl.ds(pl.multiple_of(n * (HEADS * CHUNK) + k * CHUNK, CHUNK), CHUNK)
            done[rows, lanes(k)] = (acc[at, :HEAD_WIDTH] / acc[at, HEAD_WIDTH:]).astype(jnp.bfloat16)

        @pl.when(n < CHUNKS)
        def _():
            front_copy(n).start()

        @pl.when(n == CHUNKS)
        def _():
            back_copy().start()

    kept = jnp.where(z == 3, MOVED, CHUNKS)
    tiles = jnp.where(z == 0, 16, 8 * kept)

    def own_rows(met):
        return pl.ds(pl.multiple_of((2 * met + g) * OWN, 16), OWN)

    def decode_copy(s, met, to, core, i):
        rows = own_rows(met)
        return pltpu.make_async_remote_copy(
            src_ref=dall.at[rows], dst_ref=dall.at[rows], send_sem=d_send.at[i, s], recv_sem=d_recv.at[i, s],
            device_id=(to, h, core), device_id_type=MESH,
        )

    def decode_direct(s):
        return decode_copy(s, c, met_at(s), g, 0)

    def decode_came(s):
        return decode_copy(s, met_at(s), c, other, 0)

    def decode_forward(s):
        return decode_copy(s, met_at(s), c, other, 1)

    def finish_decode():
        for k in range(HEADS):
            at = pl.ds(k * OWN, OWN)
            dall[own_rows(c), lanes(k)] = (dacc[at, :HEAD_WIDTH] / dacc[at, HEAD_WIDTH:]).astype(jnp.bfloat16)

        def send(s, carry):
            decode_direct(s).start()
            return carry

        lax.fori_loop(1, 8, send, 0)
        decode_forward(0).start()

    def in_turn(k):
        return jnp.where(k == 1, 4, jnp.where(k == 2, 1, jnp.where(k == 3, 2, jnp.where(k == 4, 6, jnp.where(k == 6, 3, k)))))

    def take(piece, carry):
        s = in_turn(piece // 2)
        for i in range(2):

            @pl.when(piece % 2 == i)
            def _():
                came(s, i).wait_recv()

                @pl.when(s == 4)
                def _():
                    sent(6, met_at(4), met_at(2), i).start()
                    sent(5, met_at(4), met_at(1), i).start()

                @pl.when(s == 6)
                def _():
                    sent(7, met_at(6), met_at(1), i).start()
                    sent(3, met_at(1), met_at(2), i).start()

                forward(s, i).start()

        @pl.when((piece == 3) & (z == 3))
        def _():
            query_copy().start()

        return carry

    def tile(e):
        moved = (z == 0) & (e >= 8)
        chunk = jnp.where(moved, CHUNKS, e % kept)
        turn = jnp.where(z == 0, jnp.where(e < 4, 0, jnp.where(e < 8, 2, e - 8)), e // kept)
        pair = met_at(in_turn(turn))
        end = jnp.where(moved, mirror, c)

        @pl.when(pair < end)
        def _():
            fold_chunk(chunk, pair, PAIR, False)

        @pl.when(pair == end)
        def _():
            fold_diagonal(chunk)

    def by_step(k, counts):
        found = counts[-1]
        for i in range(len(counts) - 1):
            found = jnp.where(k == i, counts[i], found)
        return found

    def done_until(k):
        return jnp.where(z % 3 != 1, by_step(k, (1, 2, 2, 3, 6)), by_step(k, (1, 2, 2, 3, 10)))

    def step(k, carry):
        lax.fori_loop(by_step(k, (2, 2, 3, 8, 9, 10)), by_step(k, (2, 3, 8, 9, 10, 16)), take, 0)

        def decode(n, inner):
            s = in_turn(n)
            for i in range(2):
                forward(s, i).wait_recv()
            fold_decode(met_at(s))
            return inner

        lax.fori_loop(by_step(k, (0, 1, 1, 4, 4, 5)), by_step(k, (1, 1, 4, 4, 5, 8)), decode, 0)

        @pl.when(k == 5)
        def _():
            finish_decode()

        def one(e, inner):
            tile(e)
            return inner

        lax.fori_loop(jnp.where(k == 0, 0, done_until(k - 1)), done_until(k), one, 0)
        return carry

    lax.fori_loop(0, 6, step, 0)

    @pl.when(z == 0)
    def _():
        query_copy().wait_recv()

    def part_copy(s):
        to = (h + s) % 8
        return pltpu.make_async_remote_copy(
            src_ref=part.at[pl.ds(pl.multiple_of(to * 96, 32), 96)], dst_ref=parts.at[s],
            send_sem=part_send.at[s], recv_sem=part_recv.at[s],
            device_id=(c, to, g), device_id_type=MESH,
        )

    def hand_on():
        def one(s, carry):
            decode_came(s).wait_recv()
            decode_forward(s).start()
            return carry

        lax.fori_loop(1, 8, one, 0)

    def project():
        def arrived(s, carry):
            decode_forward(s).wait_recv()
            return carry

        lax.fori_loop(0, 8, arrived, 0)
        for n in range(2):
            part[:, n * 256 : (n + 1) * 256] = jnp.dot(
                dall[...], w_ref[:, n * 256 : (n + 1) * 256], preferred_element_type=jnp.float32
            ).astype(jnp.bfloat16)

        def send(s, carry):
            part_copy(s).start()
            return carry

        lax.fori_loop(1, 8, send, 0)

    hand_on_at = by_step(z, (12, 25, 21 - 4 * xh, 13))
    project_at = by_step(z, (14, 27, 23 - 3 * xh, 16))

    def rest(e, carry):
        @pl.when(e == hand_on_at)
        def _():
            hand_on()

        @pl.when(e == project_at)
        def _():
            project()

        tile(e)
        return carry

    lax.fori_loop(done_until(5), tiles, rest, 0)

    @pl.when(z == 0)
    def _():
        finish_chunk(CHUNKS)

    def finish(n, carry):
        finish_chunk(n)
        return carry

    lax.fori_loop(0, kept, finish, 0)

    def add(s, carry):
        part_copy(s).wait_recv()
        return carry

    lax.fori_loop(1, 8, add, 0)
    total = part[pl.ds(pl.multiple_of(h * 96, 32), 96), :].astype(jnp.float32)
    for s in range(1, 8):
        total = total + parts[s].astype(jnp.float32)
    mix_ref[...] = total.astype(jnp.bfloat16)

    for n in range(MOVED):
        front_copy(n).wait()

    @pl.when(z < 3)
    def _():
        front_copy(MOVED).wait()

    @pl.when(z == 3)
    def _():
        query_copy().wait_send()
        back_copy().wait_recv()

    @pl.when(z == 0)
    def _():
        back_copy().wait_send()

    def drain(s, carry):
        for i in range(2):
            forward(s, i).wait_send()
        decode_forward(s).wait_send()

        @pl.when(s > 0)
        def _():
            for i in range(2):
                came(s, i).wait_send()
            decode_came(s).wait_send()
            part_copy(s).wait_send()

        return carry

    lax.fori_loop(0, 8, drain, 0)


def local(q, k, v, dq, prefix_len, w):
    anywhere = pl.BlockSpec(memory_space=pl.ANY)
    dma = pltpu.SemaphoreType.DMA
    bf16, f32 = jnp.bfloat16, jnp.float32
    return pl.pallas_call(
        kernel,
        out_shape=(
            jax.ShapeDtypeStruct((BLOCK, HEADS * HEAD_WIDTH), bf16),
            jax.ShapeDtypeStruct((96, 512), bf16),
        ),
        in_specs=[anywhere] * 4 + [pl.BlockSpec(memory_space=pltpu.SMEM), anywhere],
        out_specs=(anywhere, pl.BlockSpec(memory_space=pltpu.VMEM)),
        scratch_shapes=[
            pltpu.VMEM((BLOCK + CHUNK, HEADS * HEAD_WIDTH), bf16),
            pltpu.VMEM((PROMPT, HEAD_WIDTH), bf16),
            pltpu.VMEM((PROMPT, 2 * HEAD_WIDTH), bf16),
            pltpu.VMEM(((BLOCK + CHUNK) * HEADS, 2 * HEAD_WIDTH), f32),
            pltpu.VMEM(((BLOCK + CHUNK) * HEADS, HEAD_WIDTH), f32),
            pltpu.VMEM((OWN * HEADS, 2 * HEAD_WIDTH), f32),
            pltpu.VMEM((OWN * HEADS, HEAD_WIDTH), f32),
            pltpu.VMEM((BLOCK + CHUNK, HEADS * HEAD_WIDTH), bf16),
            pltpu.VMEM((CONT, HEADS * HEAD_WIDTH), bf16),
            pltpu.VMEM((CONT, 512), bf16),
            pltpu.VMEM((8, 96, 512), bf16),
            pltpu.VMEM((OWN, HEADS * HEAD_WIDTH), bf16),
            pltpu.VMEM((OWN, HEAD_WIDTH), jnp.int32),
            pltpu.VMEM((HEADS * HEAD_WIDTH, 512), bf16),
            dma((5,)),
            dma((2, 8)), dma((2, 8)), dma((2, 8)), dma((2, 8)),
            dma, dma, dma, dma, dma((CHUNKS,)),
            dma((2, 8)), dma((2, 8)), dma((8,)), dma((8,)),
        ],
        compiler_params=pltpu.CompilerParams(
            collective_id=0, has_side_effects=True, vmem_limit_bytes=56 << 20
        ),
    )(q, k, v, dq, prefix_len, w)


def solution(mesh):
    in_specs = (
        P(("ctx", "grp"), "head"),
        P(("ctx", "grp"), "head"),
        P(("ctx", "grp"), "head"),
        P(("ctx", "grp"), "head"),
        P(),
        P("head", ("ctx", "grp")),
    )
    out_specs = (P(("ctx", "grp"), "head"), P("head", ("ctx", "grp")))
    return jax.shard_map(local, mesh=mesh, in_specs=in_specs, out_specs=out_specs, check_vma=False)
```

```python
import math

import jax
import jax.numpy as jnp
from jax import lax
from jax.experimental import pallas as pl
from jax.experimental.pallas import tpu as pltpu
from jax.sharding import PartitionSpec as P

MESH = pl.DeviceIdType.MESH
HEAD_WIDTH = 128
HEADS = 8
BLOCK = 512
PAIR = 2 * BLOCK
CHUNK = 128
CHUNKS = BLOCK // CHUNK
MOVED = CHUNKS - 1
PROMPT = 8192
CONT = 768
OWN = 48
NEG = -1e30
FACTOR = HEAD_WIDTH**-0.5 * math.log2(math.e)


def lanes(h):
    return pl.ds(h * HEAD_WIDTH, HEAD_WIDTH)


def fold(queries, keys, values, limits, base, states):
    width = keys.shape[0]
    scores = [
        lax.dot_general(q, keys, (((1,), (1,)), ((), ())), preferred_element_type=jnp.float32)
        for q in queries
    ]
    results = []
    for s, limit, (m_old, acc_old) in zip(scores, limits, states):
        if limit is not None:
            place = lax.broadcasted_iota(jnp.int32, s.shape, 1)
            if limit.shape[1] != width:
                limit = jnp.concatenate([limit] * (width // limit.shape[1]), axis=1)
            s = jnp.where(place < limit - base, s, NEG)
        m_new = jnp.maximum(m_old, jnp.max(s, axis=1, keepdims=True))
        wide = jnp.concatenate([m_new] * (width // HEAD_WIDTH), axis=1)
        p = jnp.exp2((s - wide) * FACTOR).astype(jnp.bfloat16)
        shrink = jnp.exp2((m_old - m_new) * FACTOR)
        o = jnp.dot(p, values, preferred_element_type=jnp.float32)
        results.append((m_new, acc_old * jnp.concatenate([shrink, shrink], axis=1) + o))
    return results


def kernel(
    q_ref, k_ref, v_ref, dq_hbm, len_ref, w_hbm,
    ctx_ref, mix_ref,
    qall, kall, vall, acc, mx, dacc, dmx, done, dall, part, parts, dq_ref, lens, w_ref,
    load_sem, direct_send, direct_recv, forward_send, forward_recv,
    q_send, q_recv, back_send, back_recv, front_sem,
    d_send, d_recv, part_send, part_recv,
):
    c, h, g = lax.axis_index("ctx"), lax.axis_index("head"), lax.axis_index("grp")
    z, xh = c // 2, c % 2
    other = 1 - g
    mirror = 2 * (3 - z) + xh

    def met_at(s):
        flip, turn = s % 2, s // 2
        z_met = jnp.where(
            turn == 0, z, jnp.where(turn == 1, z + 1 - 2 * (z % 2), jnp.where(turn == 2, 3 - z, (z + 2) % 4))
        )
        x_met = jnp.where(flip == 0, xh, 1 - xh)
        return 2 * z_met + x_met

    barrier = pltpu.get_barrier_semaphore()

    def greet(s, carry):
        pl.semaphore_signal(barrier, inc=1, device_id=(met_at(s), h, g), device_id_type=MESH)
        pl.semaphore_signal(barrier, inc=1, device_id=(c, (h + s) % 8, g), device_id_type=MESH)
        return carry

    pl.semaphore_signal(barrier, inc=1, device_id=(c, h, other), device_id_type=MESH)
    pl.semaphore_signal(barrier, inc=1, device_id=(mirror, h, other), device_id_type=MESH)
    lax.fori_loop(1, 8, greet, 0)

    mine = pl.ds(pl.multiple_of(c * PAIR + g * BLOCK, BLOCK), BLOCK)
    front = pl.ds(0, BLOCK)
    loads = [
        pltpu.make_async_copy(src, dst, load_sem.at[i])
        for i, (src, dst) in enumerate(
            (
                (k_ref, kall.at[mine]),
                (v_ref, vall.at[mine, pl.ds(0, HEAD_WIDTH)]),
                (dq_hbm, dq_ref),
                (q_ref, qall.at[front]),
                (w_hbm, w_ref),
            )
        )
    ]
    for copy in loads:
        copy.start()
    vall[:, HEAD_WIDTH:] = jnp.ones((PROMPT, HEAD_WIDTH), jnp.bfloat16)
    acc[...] = jnp.zeros_like(acc)
    mx[...] = jnp.full_like(mx, NEG)
    dacc[...] = jnp.zeros_like(dacc)
    dmx[...] = jnp.full_like(dmx, NEG)
    for copy in loads[:2]:
        copy.wait()
    pl.semaphore_wait(barrier, 16)

    def rows_of(met):
        return pl.ds(pl.multiple_of(met * PAIR + g * BLOCK, BLOCK), BLOCK)

    def copy_of(i, rows, to, core, send, recv, s):
        ref = kall.at[rows] if i == 0 else vall.at[rows, pl.ds(0, HEAD_WIDTH)]
        return pltpu.make_async_remote_copy(
            src_ref=ref, dst_ref=ref, send_sem=send.at[i, s], recv_sem=recv.at[i, s],
            device_id=(to, h, core), device_id_type=MESH,
        )

    def sent(s, origin, to, i):
        return copy_of(i, rows_of(origin), to, g, direct_send, direct_recv, s)

    def came(s, i):
        return copy_of(i, rows_of(met_at(s)), c, other, direct_send, direct_recv, s)

    def forward(s, i):
        return copy_of(i, rows_of(met_at(s)), c, other, forward_send, forward_recv, s)

    def query_copy():
        return pltpu.make_async_remote_copy(
            src_ref=q_ref.at[pl.ds(MOVED * CHUNK, CHUNK)], dst_ref=qall.at[pl.ds(BLOCK, CHUNK)], send_sem=q_send, recv_sem=q_recv,
            device_id=(mirror, h, other), device_id_type=MESH,
        )

    for i in range(2):
        for s in (4, 1, 2):
            sent(s, c, met_at(s), i).start()
    for i in range(2):
        forward(0, i).start()

    base = (2 * c + g) * OWN
    for n in range(OWN // 8):
        row = lax.broadcasted_iota(jnp.int32, (8, HEAD_WIDTH), 0)
        value = jnp.zeros((8, HEAD_WIDTH), jnp.int32)
        for r in range(8):
            value = jnp.where(row == r, len_ref[base + n * 8 + r], value)
        lens[n * 8 : n * 8 + 8, :] = value
    for copy in loads[2:]:
        copy.wait()

    def owner(n):
        front = n < CHUNKS
        return jnp.where(front, c, mirror), jnp.where(front, g, other)

    def chunk_state(n, t):
        return pl.ds(pl.multiple_of(n * (HEADS * CHUNK) + t * (HEADS * CHUNK // 2), 512), HEADS * CHUNK // 2)

    def fold_chunk(n, pair, width, diagonal):
        rows = pl.ds(pl.multiple_of(n * CHUNK, CHUNK), CHUNK)
        span = pl.ds(pl.multiple_of(pair * PAIR, PAIR), width)
        queries = [
            jnp.concatenate([qall[rows, lanes(4 * t + k)] for k in range(4)], axis=0) for t in range(2)
        ]
        if diagonal:
            start = owner(n)[1] * BLOCK + jnp.where(n == CHUNKS, MOVED, n) * CHUNK + 1
            limit = start + lax.broadcasted_iota(jnp.int32, (512, width), 0) % CHUNK
            limits = [limit, limit]
        else:
            limits = [None, None]
        places = [chunk_state(n, t) for t in range(2)]
        states = [(mx[at, :], acc[at, :]) for at in places]
        results = fold(queries, kall[span, :], vall[span, :], limits, 0, states)
        for at, (m_new, acc_new) in zip(places, results):
            mx[at, :] = m_new
            acc[at, :] = acc_new

    def fold_diagonal(n):
        pair, core = owner(n)
        quarter = 2 * core + jnp.where(n == CHUNKS, MOVED, n) // 2
        for k in range(4):

            @pl.when(quarter == k)
            def _():
                fold_chunk(n, pair, (k + 1) * 2 * CHUNK, True)

    def fold_decode(pair):
        span = pl.ds(pl.multiple_of(pair * PAIR, PAIR), PAIR)
        queries = [
            jnp.concatenate([dq_ref[:, lanes(4 * t + k)] for k in range(4)], axis=0) for t in range(2)
        ]
        limit = jnp.concatenate([lens[...]] * 4, axis=0)
        places = [pl.ds(t * 4 * OWN, 4 * OWN) for t in range(2)]
        states = [(dmx[at, :], dacc[at, :]) for at in places]
        results = fold(queries, kall[span, :], vall[span, :], [limit, limit], pair * PAIR, states)
        for at, (m_new, acc_new) in zip(places, results):
            dmx[at, :] = m_new
            dacc[at, :] = acc_new

    def back_copy():
        return pltpu.make_async_remote_copy(
            src_ref=done.at[pl.ds(BLOCK, CHUNK)], dst_ref=ctx_ref.at[pl.ds(MOVED * CHUNK, CHUNK)], send_sem=back_send, recv_sem=back_recv,
            device_id=(mirror, h, other), device_id_type=MESH,
        )

    def front_copy(n):
        rows = pl.ds(pl.multiple_of(n * CHUNK, CHUNK), CHUNK)
        return pltpu.make_async_copy(done.at[rows], ctx_ref.at[rows], front_sem.at[n])

    def finish_chunk(n):
        rows = pl.ds(pl.multiple_of(n * CHUNK, CHUNK), CHUNK)
        for k in range(HEADS):
            at = pl.ds(pl.multiple_of(n * (HEADS * CHUNK) + k * CHUNK, CHUNK), CHUNK)
            done[rows, lanes(k)] = (acc[at, :HEAD_WIDTH] / acc[at, HEAD_WIDTH:]).astype(jnp.bfloat16)

        @pl.when(n < CHUNKS)
        def _():
            front_copy(n).start()

        @pl.when(n == CHUNKS)
        def _():
            back_copy().start()

    kept = jnp.where(z == 3, MOVED, CHUNKS)
    tiles = jnp.where(z == 0, 16, 8 * kept)

    def own_rows(met):
        return pl.ds(pl.multiple_of((2 * met + g) * OWN, 16), OWN)

    def decode_copy(s, met, to, core, i):
        rows = own_rows(met)
        return pltpu.make_async_remote_copy(
            src_ref=dall.at[rows], dst_ref=dall.at[rows], send_sem=d_send.at[i, s], recv_sem=d_recv.at[i, s],
            device_id=(to, h, core), device_id_type=MESH,
        )

    def decode_direct(s):
        return decode_copy(s, c, met_at(s), g, 0)

    def decode_came(s):
        return decode_copy(s, met_at(s), c, other, 0)

    def decode_forward(s):
        return decode_copy(s, met_at(s), c, other, 1)

    def finish_decode():
        for k in range(HEADS):
            at = pl.ds(k * OWN, OWN)
            dall[own_rows(c), lanes(k)] = (dacc[at, :HEAD_WIDTH] / dacc[at, HEAD_WIDTH:]).astype(jnp.bfloat16)

        def send(s, carry):
            decode_direct(s).start()
            return carry

        lax.fori_loop(1, 8, send, 0)
        decode_forward(0).start()

    def in_turn(k):
        return jnp.where(k == 1, 4, jnp.where(k == 2, 1, jnp.where(k == 3, 2, jnp.where(k == 4, 6, jnp.where(k == 6, 3, k)))))

    def take(piece, carry):
        s = in_turn(piece // 2)
        for i in range(2):

            @pl.when(piece % 2 == i)
            def _():
                came(s, i).wait_recv()

                @pl.when(s == 4)
                def _():
                    sent(6, met_at(4), met_at(2), i).start()
                    sent(5, met_at(4), met_at(1), i).start()

                @pl.when(s == 6)
                def _():
                    sent(7, met_at(6), met_at(1), i).start()
                    sent(3, met_at(1), met_at(2), i).start()

                forward(s, i).start()

        @pl.when((piece == 3) & (z == 3))
        def _():
            query_copy().start()

        return carry

    def tile(e):
        moved = (z == 0) & (e >= 8)
        chunk = jnp.where(moved, CHUNKS, e % kept)
        turn = jnp.where(z == 0, jnp.where(e < 4, 0, jnp.where(e < 8, 2, e - 8)), e // kept)
        pair = met_at(in_turn(turn))
        end = jnp.where(moved, mirror, c)

        @pl.when(pair < end)
        def _():
            fold_chunk(chunk, pair, PAIR, False)

        @pl.when(pair == end)
        def _():
            fold_diagonal(chunk)

    def by_step(k, counts):
        found = counts[-1]
        for i in range(len(counts) - 1):
            found = jnp.where(k == i, counts[i], found)
        return found

    def done_until(k):
        return jnp.where(
            z >= 2,
            by_step(k, (1, 2, 2, 3, 6)),
            jnp.where(z == 1, by_step(k, (1, 2, 2, 3, 10)), by_step(k, (1, 2, 2, 3, 6))),
        )

    def step(k, carry):
        lax.fori_loop(by_step(k, (2, 2, 3, 8, 9, 10)), by_step(k, (2, 3, 8, 9, 10, 16)), take, 0)

        def decode(n, inner):
            s = in_turn(n)
            for i in range(2):
                forward(s, i).wait_recv()
            fold_decode(met_at(s))
            return inner

        lax.fori_loop(by_step(k, (0, 1, 1, 4, 4, 5)), by_step(k, (1, 1, 4, 4, 5, 8)), decode, 0)

        @pl.when(k == 5)
        def _():
            finish_decode()

        def one(e, inner):
            tile(e)
            return inner

        lax.fori_loop(jnp.where(k == 0, 0, done_until(k - 1)), done_until(k), one, 0)
        return carry

    lax.fori_loop(0, 6, step, 0)

    @pl.when(z == 0)
    def _():
        query_copy().wait_recv()

    def part_copy(s):
        to = (h + s) % 8
        return pltpu.make_async_remote_copy(
            src_ref=part.at[pl.ds(pl.multiple_of(to * 96, 32), 96)], dst_ref=parts.at[s],
            send_sem=part_send.at[s], recv_sem=part_recv.at[s],
            device_id=(c, to, g), device_id_type=MESH,
        )

    def hand_on():
        def one(s, carry):
            decode_came(s).wait_recv()
            decode_forward(s).start()
            return carry

        lax.fori_loop(1, 8, one, 0)

    def project():
        def arrived(s, carry):
            decode_forward(s).wait_recv()
            return carry

        lax.fori_loop(0, 8, arrived, 0)
        for n in range(2):
            part[:, n * 256 : (n + 1) * 256] = jnp.dot(
                dall[...], w_ref[:, n * 256 : (n + 1) * 256], preferred_element_type=jnp.float32
            ).astype(jnp.bfloat16)

        def send(s, carry):
            part_copy(s).start()
            return carry

        lax.fori_loop(1, 8, send, 0)

    hand_on_at = by_step(z, (12, 25, 21 - 2 * xh, 15))
    project_at = by_step(z, (14, 27, 28 - 6 * xh, 18))

    def rest(e, carry):
        @pl.when(e == hand_on_at)
        def _():
            hand_on()

        @pl.when(e == project_at)
        def _():
            project()

        tile(e)
        return carry

    lax.fori_loop(done_until(5), tiles, rest, 0)

    @pl.when(z == 0)
    def _():
        finish_chunk(CHUNKS)

    def finish(n, carry):
        finish_chunk(n)
        return carry

    lax.fori_loop(0, kept, finish, 0)

    def add(s, carry):
        part_copy(s).wait_recv()
        return carry

    lax.fori_loop(1, 8, add, 0)
    total = part[pl.ds(pl.multiple_of(h * 96, 32), 96), :].astype(jnp.float32)
    for s in range(1, 8):
        total = total + parts[s].astype(jnp.float32)
    mix_ref[...] = total.astype(jnp.bfloat16)

    for n in range(MOVED):
        front_copy(n).wait()

    @pl.when(z < 3)
    def _():
        front_copy(MOVED).wait()

    @pl.when(z == 3)
    def _():
        query_copy().wait_send()
        back_copy().wait_recv()

    @pl.when(z == 0)
    def _():
        back_copy().wait_send()

    def drain(s, carry):
        for i in range(2):
            forward(s, i).wait_send()
        decode_forward(s).wait_send()

        @pl.when(s > 0)
        def _():
            for i in range(2):
                came(s, i).wait_send()
            decode_came(s).wait_send()
            part_copy(s).wait_send()

        return carry

    lax.fori_loop(0, 8, drain, 0)


def store(ctx_in, mix_in, ctx_out, mix_out, ctx, mix, sem):
    pieces = [
        (ctx_in.at[pl.ds(n * CHUNK, CHUNK)], ctx.at[pl.ds(n * CHUNK, CHUNK)], ctx_out.at[pl.ds(n * CHUNK, CHUNK)])
        for n in range(CHUNKS)
    ] + [(mix_in, mix, mix_out)]
    reads = [pltpu.make_async_copy(a, b, sem.at[0, n]) for n, (a, b, _) in enumerate(pieces)]
    writes = [pltpu.make_async_copy(b, c, sem.at[1, n]) for n, (_, b, c) in enumerate(pieces)]
    for copy in reads:
        copy.start()
    for read, write in zip(reads, writes):
        read.wait()
        write.start()
    for copy in writes:
        copy.wait()


def local(q, k, v, dq, prefix_len, w):
    anywhere = pl.BlockSpec(memory_space=pl.ANY)
    dma = pltpu.SemaphoreType.DMA
    bf16, f32 = jnp.bfloat16, jnp.float32
    results = (
        jax.ShapeDtypeStruct((BLOCK, HEADS * HEAD_WIDTH), bf16),
        jax.ShapeDtypeStruct((96, 512), bf16),
    )
    attended = pl.pallas_call(
        kernel,
        out_shape=results,
        in_specs=[anywhere] * 4 + [pl.BlockSpec(memory_space=pltpu.SMEM), anywhere],
        out_specs=(anywhere, pl.BlockSpec(memory_space=pltpu.VMEM)),
        scratch_shapes=[
            pltpu.VMEM((BLOCK + CHUNK, HEADS * HEAD_WIDTH), bf16),
            pltpu.VMEM((PROMPT, HEAD_WIDTH), bf16),
            pltpu.VMEM((PROMPT, 2 * HEAD_WIDTH), bf16),
            pltpu.VMEM(((BLOCK + CHUNK) * HEADS, 2 * HEAD_WIDTH), f32),
            pltpu.VMEM(((BLOCK + CHUNK) * HEADS, HEAD_WIDTH), f32),
            pltpu.VMEM((OWN * HEADS, 2 * HEAD_WIDTH), f32),
            pltpu.VMEM((OWN * HEADS, HEAD_WIDTH), f32),
            pltpu.VMEM((BLOCK + CHUNK, HEADS * HEAD_WIDTH), bf16),
            pltpu.VMEM((CONT, HEADS * HEAD_WIDTH), bf16),
            pltpu.VMEM((CONT, 512), bf16),
            pltpu.VMEM((8, 96, 512), bf16),
            pltpu.VMEM((OWN, HEADS * HEAD_WIDTH), bf16),
            pltpu.VMEM((OWN, HEAD_WIDTH), jnp.int32),
            pltpu.VMEM((HEADS * HEAD_WIDTH, 512), bf16),
            dma((5,)),
            dma((2, 8)), dma((2, 8)), dma((2, 8)), dma((2, 8)),
            dma, dma, dma, dma, dma((CHUNKS,)),
            dma((2, 8)), dma((2, 8)), dma((8,)), dma((8,)),
        ],
        compiler_params=pltpu.CompilerParams(
            collective_id=0, has_side_effects=True, vmem_limit_bytes=56 << 20
        ),
    )(q, k, v, dq, prefix_len, w)
    return pl.pallas_call(
        store,
        out_shape=results,
        in_specs=[anywhere] * 2,
        out_specs=(anywhere, anywhere),
        scratch_shapes=[
            pltpu.VMEM((BLOCK, HEADS * HEAD_WIDTH), bf16),
            pltpu.VMEM((96, 512), bf16),
            dma((2, CHUNKS + 1)),
        ],
    )(*attended)


def solution(mesh):
    in_specs = (
        P(("ctx", "grp"), "head"),
        P(("ctx", "grp"), "head"),
        P(("ctx", "grp"), "head"),
        P(("ctx", "grp"), "head"),
        P(),
        P("head", ("ctx", "grp")),
    )
    out_specs = (P(("ctx", "grp"), "head"), P("head", ("ctx", "grp")))
    return jax.shard_map(local, mesh=mesh, in_specs=in_specs, out_specs=out_specs, check_vma=False)
```
